32 devices in a mesh: groups: 2 (over y), row: 4 (over z), col: 4 (over x, core).
Axes of the slice: x: 2, y: 2, z: 4, core: 2. Of those that a mesh axis runs over, the one named last changes fastest.
Arguments:
- row_embed: bfloat16 [8, 256, 1024], P(('groups', 'row'), 'col'), parts along dimension 0, may hold values from -6 to 6
- col_embed: bfloat16 [8, 256, 1024], P(('groups', 'col'), 'row'), parts along dimension 0, may hold values from -6 to 6
- pos_rows: int32 [8, 4, 256], P(('groups', 'row'), 'col'), parts along dimension 0, may hold values from 0 to 255
- pos_cols: int32 [8, 4, 256], P(('groups', 'row'), 'col'), parts along dimension 0, may hold values from 0 to 255
- logit_scale: float32 [1], replicated, may hold values from 0.06 to 0.1
- logit_bias: float32 [1], replicated, may hold values from -9 to -7
Outputs:
- logits: bfloat16 [2048, 1024], P(('groups', 'row'), 'col'), parts along dimension 0
- row_grad: bfloat16 [8, 256, 1024], P(('groups', 'row'), 'col'), parts along dimension 0
- col_grad: bfloat16 [8, 256, 1024], P(('groups', 'col'), 'row'), parts along dimension 0
The draws below stay inside these ranges and needn't reach their ends.
There are 2 independent parts, one for each index of `groups`. The reference program is written for one: setup_inputs(seed, part) draws one part's arguments, and reference() takes and returns one part's arrays. A program takes and returns all parts, laid end to end along the dimension named above; an argument that names none is the same for every part. Nothing has to cross between parts.
Inputs may be any that keep to these rules, and one draw needn't show every extreme that they name: `pos_rows`: indices are local to the tile; a pair listed twice counts once. `pos_cols`: indices are local to the tile and match pos_rows entry by entry.
All inputs are finite; a program needn't handle non-finite values.
Results may differ from the reference program's by a relative error of at most 0.012.
Values may be sent and summed in bfloat16 or wider, within the bound.
A program may use at most 64 MiB of HBM per device.

```python
import jax
import jax.numpy as jnp
from jax import lax

D = 1024
ROWS_TILE = 256
COLS_TILE = 256
PAIRS = 256
N_ROW = 4
N_COL = 4


def place_ends(values, rng, low, top_value):
    spot = [jax.random.randint(jax.random.fold_in(rng, axis), (), 0, length) for axis, length in enumerate(values.shape)]
    longest = values.shape.index(max(values.shape))
    neighbour = spot[:longest] + [(spot[longest] + 1) % values.shape[longest]] + spot[longest + 1:]
    return values.at[tuple(spot)].set(low).at[tuple(neighbour)].set(top_value)


def shard_levels(rng, dims, pieces, low, high):
    factor_of, own = 1.0, jax.random.fold_in(rng, 6)
    for axis_at, shards_of in pieces:
        heights = jnp.exp(jax.random.uniform(jax.random.fold_in(own, axis_at), (shards_of,), jnp.float32, low / len(pieces), high / len(pieces)))
        factor_of = factor_of * jnp.repeat(heights, dims[axis_at] // shards_of).reshape([-1 if axis == axis_at else 1 for axis in range(len(dims))])
    return factor_of


def centred(own_key, dims, deviation, bound, cuts=(), held_as=jnp.bfloat16):
    gain = shard_levels(own_key, dims, cuts, -0.22, 0.18) if cuts else 1.0
    values = jax.random.normal(own_key, dims, jnp.float32) * deviation * gain
    return jnp.minimum(jnp.maximum(values, -bound), bound).astype(held_as)


def setup_inputs(seed: int = 0, part: int = 0) -> dict:
    splits = jax.random.split(jax.random.key(seed), 7)
    own_keys = jax.random.split(jax.random.fold_in(splits[6], part), 7)
    return {
        "row_embed": centred(own_keys[0], (N_ROW, ROWS_TILE, D), 1.0, 6.0, ((0, 4), (1, 4))),
        "col_embed": centred(own_keys[1], (N_COL, COLS_TILE, D), 1.0, 6.0, ((0, 4), (1, 4))),
        "pos_rows": place_ends(jax.random.randint(own_keys[2], (N_ROW, N_COL, PAIRS), 0, ROWS_TILE), jax.random.fold_in(own_keys[2], 1), 0, ROWS_TILE - 1).astype(jnp.int32),
        "pos_cols": place_ends(jax.random.randint(own_keys[3], (N_ROW, N_COL, PAIRS), 0, COLS_TILE), jax.random.fold_in(own_keys[3], 1), 0, COLS_TILE - 1).astype(jnp.int32),
        "logit_scale": jnp.clip(jax.random.uniform(splits[4], (1,), jnp.float32, 0.06, 0.1), 0.06, 0.1),
        "logit_bias": jnp.clip(jax.random.uniform(splits[5], (1,), jnp.float32, -9.0, -7.0), -9.0, -7.0),
    }


def reference(row_embed, col_embed, pos_rows, pos_cols, logit_scale, logit_bias):
    n_rows, rows_tile, features = row_embed.shape
    n_cols, cols_tile, _ = col_embed.shape
    factor = logit_scale[0]
    offset = logit_bias[0]
    col_all = col_embed.reshape(n_cols * cols_tile, features)
    col_wide = col_embed.astype(jnp.float32)
    col_starts = (jnp.arange(n_cols, dtype=jnp.int32) * cols_tile)[:, None]

    def step(running, inputs):
        row_block, rows_index, cols_index = inputs
        scores = factor * jnp.dot(row_block, col_all.T, preferred_element_type=jnp.float32) + offset
        labels = jnp.zeros((rows_tile, n_cols * cols_tile), jnp.float32)
        labels = labels.at[rows_index.reshape(-1), (cols_index + col_starts).reshape(-1)].max(1.0)
        grad_tile = (jax.nn.sigmoid(scores) - labels).astype(jnp.bfloat16)
        tiles = grad_tile.astype(jnp.float32).reshape(rows_tile, n_cols, cols_tile)
        row_parts = jnp.einsum("rcj,cjd->crd", tiles, col_wide).astype(jnp.bfloat16)
        row_parts = lax.optimization_barrier(row_parts).astype(jnp.float32)
        row_out = (factor * jnp.sum(row_parts, axis=0)).astype(jnp.bfloat16)
        col_parts = jnp.einsum("rcj,rd->cjd", tiles, row_block.astype(jnp.float32)).astype(jnp.bfloat16)
        col_parts = lax.optimization_barrier(col_parts).astype(jnp.float32)
        return running + col_parts, (scores.astype(jnp.bfloat16), row_out)

    start_sum = jnp.zeros((n_cols, cols_tile, features), jnp.float32)
    col_total, (logit_rows, row_grad) = lax.scan(step, start_sum, (row_embed, pos_rows, pos_cols))
    logits = logit_rows.reshape(n_rows * rows_tile, n_cols * cols_tile)
    col_grad = (factor * col_total).astype(jnp.bfloat16)
    return (logits, row_grad, col_grad)
```

```python
import functools

import jax
import jax.numpy as jnp
from jax import lax
from jax.experimental import pallas as pl
from jax.experimental.pallas import tpu as pltpu
from jax.sharding import PartitionSpec as P

NT = (((1,), (1,)), ((), ()))


def nearest(me, n, step):
    inner = jnp.minimum(me, n - 1 - me)
    both = (step + 1) // 2 * (2 * (step % 2) - 1)
    one = (step - inner) * jnp.where(2 * me < n, 1, -1)
    return me + jnp.where(step <= 2 * inner, both, one)


def kernel(
    nr, nc, scale_ref, bias_ref, pr_ref, pc_ref, row_ref, col_ref,
    logit_out, row_out, col_out,
    rows, cols, labels, lt, gt, logit_v, cp, cp_in, rp, rp_in, row_v, col_v,
    own_sem, out_sem, row_send, row_recv, col_send, col_recv, cp_send, cp_recv, rp_send, rp_recv,
):
    g, r, c = lax.axis_index("groups"), lax.axis_index("row"), lax.axis_index("col")
    rs, cs = row_ref.shape[1], col_ref.shape[1]
    depth = row_ref.shape[2]
    rows_tile, cols_tile = rs * nc, cs * nr

    barrier = pltpu.get_barrier_semaphore()
    for k in range(1, nr):
        pl.semaphore_signal(barrier, inc=1, device_id=(g, lax.rem(r + k, nr), c), device_id_type=pl.DeviceIdType.MESH)
    for k in range(1, nc):
        pl.semaphore_signal(barrier, inc=1, device_id=(g, r, lax.rem(c + k, nc)), device_id_type=pl.DeviceIdType.MESH)
    own_row = pltpu.make_async_copy(row_ref.at[0], rows.at[c], own_sem.at[0])
    own_col = pltpu.make_async_copy(col_ref.at[0], cols.at[r], own_sem.at[1])
    own_row.start()
    own_col.start()

    def remote(src, dst, send, recv, where):
        return pltpu.make_async_remote_copy(
            src_ref=src, dst_ref=dst, send_sem=send, recv_sem=recv, device_id=where, device_id_type=pl.DeviceIdType.MESH
        )

    def row_copy(k, slot):
        return remote(row_ref.at[0], rows.at[slot], row_send.at[k], row_recv.at[slot], (g, r, lax.rem(c + k, nc)))

    def col_copy(peer, slot):
        return remote(col_ref.at[0], cols.at[slot], col_send.at[peer], col_recv.at[slot], (g, peer, c))

    def cp_copy(peer, slot):
        return remote(cp.at[peer], cp_in.at[slot], cp_send.at[peer], cp_recv.at[slot], (g, peer, c))

    def rp_copy(peer, slot):
        return remote(rp.at[peer], rp_in.at[slot], rp_send.at[peer], rp_recv.at[slot], (g, r, peer))

    pl.semaphore_wait(barrier, nr + nc - 2)
    for k in range(1, nr):
        col_copy(nearest(r, nr, k), r).start()
    for k in range(1, nc):
        row_copy(k, c).start()

    factor, offset = scale_ref[0], bias_ref[0]
    pairs = pr_ref.shape[2]
    hit_rows = (lax.broadcasted_iota(jnp.int32, (rows_tile, pairs), 0) == pr_ref[0]).astype(jnp.bfloat16)
    hit_cols = (lax.broadcasted_iota(jnp.int32, (cols_tile, pairs), 0) == pc_ref[0]).astype(jnp.bfloat16)
    count = lax.dot_general(hit_cols, hit_rows, NT, preferred_element_type=jnp.float32)
    labels[...] = jnp.where(count > 0.5, 1.0, 0.0)

    own_row.wait()
    own_col.wait()
    for k in range(1, nc):
        row_copy(k, lax.rem(c + k, nc)).wait_recv()

    def block(s):
        at = pl.ds(pl.multiple_of(s * cs, cs), cs)
        row_all = rows[...].reshape(rows_tile, depth)
        scores = factor * lax.dot_general(cols[s], row_all, NT, preferred_element_type=jnp.float32) + offset
        lt[at, :] = scores
        grad = (jax.nn.sigmoid(scores) - labels[at, :]).astype(jnp.bfloat16)
        gt[at, :] = grad
        return jnp.dot(grad, row_all, preferred_element_type=jnp.float32).astype(jnp.bfloat16)

    cp_in[r] = block(r)

    def arrived(k):
        s = nearest(r, nr, k)
        col_copy(s, s).wait_recv()
        cp[s] = block(s)
        cp_copy(s, r).start()

    if nr <= 4:
        for k in range(1, nr):
            arrived(k)
    else:
        pl.loop(1, nr)(arrived)

    cols_all = cols[...].reshape(cols_tile, depth)
    grad = gt[...].T
    out = jnp.dot(grad, cols_all, preferred_element_type=jnp.float32).astype(jnp.bfloat16)
    rp[...] = out.reshape(nc, rs, depth)
    for k in range(1, nc):
        rp_copy(lax.rem(c + k, nc), c).start()
    rp_in[c] = rp[c]
    logit_v[...] = lt[...].T.astype(jnp.bfloat16)
    logit_copy = pltpu.make_async_copy(logit_v, logit_out, out_sem.at[0])
    logit_copy.start()

    def total(parts, n):
        add = parts[0].astype(jnp.float32)
        for s in range(1, n):
            add += parts[s].astype(jnp.float32)
        return (factor * add).astype(jnp.bfloat16)

    for k in range(1, nr):
        s = nearest(r, nr, k)
        cp_copy(s, s).wait_recv()
    col_v[...] = total(cp_in, nr)
    col_done = pltpu.make_async_copy(col_v, col_out.at[0], out_sem.at[1])
    col_done.start()
    for k in range(1, nc):
        s = lax.rem(c + k, nc)
        rp_copy(s, s).wait_recv()
    row_v[...] = total(rp_in, nc)
    row_done = pltpu.make_async_copy(row_v, row_out.at[0], out_sem.at[2])
    row_done.start()

    for k in range(1, nr):
        s = nearest(r, nr, k)
        col_copy(s, r).wait_send()
        cp_copy(s, r).wait_send()
    for k in range(1, nc):
        row_copy(k, c).wait_send()
        rp_copy(lax.rem(c + k, nc), c).wait_send()
    logit_copy.wait()
    col_done.wait()
    row_done.wait()


def local(nr, nc, row_embed, col_embed, pos_rows, pos_cols, logit_scale, logit_bias):
    _, rs, depth = row_embed.shape
    cs = col_embed.shape[1]
    rows_tile, cols_tile = rs * nc, cs * nr
    bf16, f32 = jnp.bfloat16, jnp.float32
    smem, vmem, hbm = (pl.BlockSpec(memory_space=m) for m in (pltpu.SMEM, pltpu.VMEM, pl.ANY))
    dma = pltpu.SemaphoreType.DMA
    return pl.pallas_call(
        functools.partial(kernel, nr, nc),
        out_shape=(
            jax.ShapeDtypeStruct((rows_tile, cols_tile), bf16),
            jax.ShapeDtypeStruct((1, rs, depth), bf16),
            jax.ShapeDtypeStruct((1, cs, depth), bf16),
        ),
        in_specs=[smem, smem, vmem, vmem, hbm, hbm],
        out_specs=(hbm, hbm, hbm),
        scratch_shapes=[
            pltpu.VMEM((nc, rs, depth), bf16),
            pltpu.VMEM((nr, cs, depth), bf16),
            pltpu.VMEM((cols_tile, rows_tile), f32),
            pltpu.VMEM((cols_tile, rows_tile), f32),
            pltpu.VMEM((cols_tile, rows_tile), bf16),
            pltpu.VMEM((rows_tile, cols_tile), bf16),
            pltpu.VMEM((nr, cs, depth), bf16),
            pltpu.VMEM((nr, cs, depth), bf16),
            pltpu.VMEM((nc, rs, depth), bf16),
            pltpu.VMEM((nc, rs, depth), bf16),
            pltpu.VMEM((rs, depth), bf16),
            pltpu.VMEM((cs, depth), bf16),
            dma((2,)),
            dma((3,)),
            dma((nc,)),
            dma((nc,)),
            dma((nr,)),
            dma((nr,)),
            dma((nr,)),
            dma((nr,)),
            dma((nc,)),
            dma((nc,)),
        ],
        compiler_params=pltpu.CompilerParams(
            collective_id=0, has_side_effects=True, vmem_limit_bytes=50 * 1024 * 1024
        ),
    )(logit_scale, logit_bias, pos_rows, pos_cols, row_embed, col_embed)


def solution(mesh):
    in_specs = (
        P(("groups", "row"), "col", None),
        P(("groups", "col"), "row", None),
        P(("groups", "row"), "col", None),
        P(("groups", "row"), "col", None),
        P(),
        P(),
    )
    out_specs = (
        P(("groups", "row"), "col"),
        P(("groups", "row"), "col", None),
        P(("groups", "col"), "row", None),
    )
    body = functools.partial(local, mesh.shape["row"], mesh.shape["col"])
    return jax.shard_map(body, mesh=mesh, in_specs=in_specs, out_specs=out_specs, check_vma=False)
```

```python
import functools

import jax
import jax.numpy as jnp
from jax import lax
from jax.experimental import pallas as pl
from jax.experimental.pallas import tpu as pltpu
from jax.sharding import PartitionSpec as P

NT = (((1,), (1,)), ((), ()))


def nearest(me, n, step):
    inner = jnp.minimum(me, n - 1 - me)
    both = (step + 1) // 2 * (2 * (step % 2) - 1)
    one = (step - inner) * jnp.where(2 * me < n, 1, -1)
    return me + jnp.where(step <= 2 * inner, both, one)


def kernel(
    nr, nc, scale_hbm, bias_hbm, pr_hbm, pc_hbm, row_ref, col_ref,
    logit_out, row_out, col_out,
    scale_ref, bias_ref, pr_ref, pc_ref, rows, cols, labels, lt, gt, cp, cp_in, rp, rp_in,
    own_sem, row_send, row_recv, col_send, col_recv, cp_send, cp_recv, rp_send, rp_recv,
):
    g, r, c = lax.axis_index("groups"), lax.axis_index("row"), lax.axis_index("col")
    rs, cs = row_ref.shape[1], col_ref.shape[1]
    depth = row_ref.shape[2]
    rows_tile, cols_tile = rs * nc, cs * nr

    barrier = pltpu.get_barrier_semaphore()
    for k in range(1, nr):
        pl.semaphore_signal(barrier, inc=1, device_id=(g, lax.rem(r + k, nr), c), device_id_type=pl.DeviceIdType.MESH)
    for k in range(1, nc):
        pl.semaphore_signal(barrier, inc=1, device_id=(g, r, lax.rem(c + k, nc)), device_id_type=pl.DeviceIdType.MESH)
    own_row = pltpu.make_async_copy(row_ref.at[0], rows.at[c], own_sem.at[0])
    own_col = pltpu.make_async_copy(col_ref.at[0], cols.at[r], own_sem.at[1])
    small = [
        pltpu.make_async_copy(src, dst, own_sem.at[2 + i])
        for i, (src, dst) in enumerate(
            ((pr_hbm, pr_ref), (pc_hbm, pc_ref), (scale_hbm, scale_ref), (bias_hbm, bias_ref))
        )
    ]
    for copy in [*small, own_row, own_col]:
        copy.start()

    def remote(src, dst, send, recv, where):
        return pltpu.make_async_remote_copy(
            src_ref=src, dst_ref=dst, send_sem=send, recv_sem=recv, device_id=where, device_id_type=pl.DeviceIdType.MESH
        )

    def row_copy(k, slot):
        return remote(row_ref.at[0], rows.at[slot], row_send.at[k], row_recv.at[slot], (g, r, lax.rem(c + k, nc)))

    def col_copy(peer, slot):
        return remote(col_ref.at[0], cols.at[slot], col_send.at[peer], col_recv.at[slot], (g, peer, c))

    def cp_copy(peer, slot):
        return remote(cp.at[peer], cp_in.at[slot], cp_send.at[peer], cp_recv.at[slot], (g, peer, c))

    def rp_copy(peer, slot):
        return remote(rp.at[peer], rp_in.at[slot], rp_send.at[peer], rp_recv.at[slot], (g, r, peer))

    pl.semaphore_wait(barrier, nr + nc - 2)
    for k in range(1, nr):
        col_copy(nearest(r, nr, k), r).start()
    for k in range(1, nc):
        row_copy(k, c).start()

    for copy in small:
        copy.wait()
    factor, offset = scale_ref[0], bias_ref[0]
    pairs = pr_ref.shape[2]
    hit_rows = (lax.broadcasted_iota(jnp.int32, (rows_tile, pairs), 0) == pr_ref[0]).astype(jnp.bfloat16)
    hit_cols = (lax.broadcasted_iota(jnp.int32, (cols_tile, pairs), 0) == pc_ref[0]).astype(jnp.bfloat16)
    count = lax.dot_general(hit_cols, hit_rows, NT, preferred_element_type=jnp.float32)
    labels[...] = jnp.where(count > 0.5, 1.0, 0.0)

    own_row.wait()
    own_col.wait()
    for k in range(1, nc):
        row_copy(k, lax.rem(c + k, nc)).wait_recv()

    def block(s):
        at = pl.ds(pl.multiple_of(s * cs, cs), cs)
        row_all = rows[...].reshape(rows_tile, depth)
        scores = factor * lax.dot_general(cols[s], row_all, NT, preferred_element_type=jnp.float32) + offset
        lt[at, :] = scores
        grad = (jax.nn.sigmoid(scores) - labels[at, :]).astype(jnp.bfloat16)
        gt[at, :] = grad
        return jnp.dot(grad, row_all, preferred_element_type=jnp.float32).astype(jnp.bfloat16)

    cp_in[r] = block(r)

    def arrived(k):
        s = nearest(r, nr, k)
        col_copy(s, s).wait_recv()
        cp[s] = block(s)
        cp_copy(s, r).start()

    if nr <= 4:
        for k in range(1, nr):
            arrived(k)
    else:
        pl.loop(1, nr)(arrived)

    cols_all = cols[...].reshape(cols_tile, depth)
    grad = gt[...].T
    out = jnp.dot(grad, cols_all, preferred_element_type=jnp.float32).astype(jnp.bfloat16)
    rp[...] = out.reshape(nc, rs, depth)
    for k in range(1, nc):
        rp_copy(lax.rem(c + k, nc), c).start()
    rp_in[c] = rp[c]
    logit_out[...] = lt[...].T.astype(jnp.bfloat16)

    def total(parts, n):
        add = parts[0].astype(jnp.float32)
        for s in range(1, n):
            add += parts[s].astype(jnp.float32)
        return (factor * add).astype(jnp.bfloat16)

    for k in range(1, nr):
        s = nearest(r, nr, k)
        cp_copy(s, s).wait_recv()
    col_out[0] = total(cp_in, nr)
    for k in range(1, nc):
        s = lax.rem(c + k, nc)
        rp_copy(s, s).wait_recv()
    row_out[0] = total(rp_in, nc)

    for k in range(1, nr):
        s = nearest(r, nr, k)
        col_copy(s, r).wait_send()
        cp_copy(s, r).wait_send()
    for k in range(1, nc):
        row_copy(k, c).wait_send()
        rp_copy(lax.rem(c + k, nc), c).wait_send()


def write_out(*refs):
    sems = refs[-1]
    held, out = refs[:3], refs[3:6]
    copies = [pltpu.make_async_copy(src, dst, sems.at[i]) for i, (src, dst) in enumerate(zip(held, out))]
    for copy in copies:
        copy.start()
    for copy in copies:
        copy.wait()


def local(nr, nc, row_embed, col_embed, pos_rows, pos_cols, logit_scale, logit_bias):
    _, rs, depth = row_embed.shape
    cs = col_embed.shape[1]
    rows_tile, cols_tile = rs * nc, cs * nr
    bf16, f32 = jnp.bfloat16, jnp.float32
    vmem, hbm = (pl.BlockSpec(memory_space=m) for m in (pltpu.VMEM, pltpu.HBM))
    dma = pltpu.SemaphoreType.DMA
    shapes = (
        jax.ShapeDtypeStruct((rows_tile, cols_tile), bf16),
        jax.ShapeDtypeStruct((1, rs, depth), bf16),
        jax.ShapeDtypeStruct((1, cs, depth), bf16),
    )
    operands = (pos_rows, pos_cols, row_embed, col_embed)
    pinned = [pltpu.with_memory_space_constraint(x, pltpu.HBM) for x in operands]
    held = pl.pallas_call(
        functools.partial(kernel, nr, nc),
        out_shape=shapes,
        in_specs=[hbm] * 6,
        out_specs=(vmem,) * 3,
        scratch_shapes=[
            pltpu.SMEM((1,), f32),
            pltpu.SMEM((1,), f32),
            pltpu.VMEM(pos_rows.shape, jnp.int32),
            pltpu.VMEM(pos_cols.shape, jnp.int32),
            pltpu.VMEM((nc, rs, depth), bf16),
            pltpu.VMEM((nr, cs, depth), bf16),
            pltpu.VMEM((cols_tile, rows_tile), f32),
            pltpu.VMEM((cols_tile, rows_tile), f32),
            pltpu.VMEM((cols_tile, rows_tile), bf16),
            pltpu.VMEM((nr, cs, depth), bf16),
            pltpu.VMEM((nr, cs, depth), bf16),
            pltpu.VMEM((nc, rs, depth), bf16),
            pltpu.VMEM((nc, rs, depth), bf16),
            dma((6,)),
            dma((nc,)),
            dma((nc,)),
            dma((nr,)),
            dma((nr,)),
            dma((nr,)),
            dma((nr,)),
            dma((nc,)),
            dma((nc,)),
        ],
        compiler_params=pltpu.CompilerParams(
            collective_id=0, has_side_effects=True, vmem_limit_bytes=50 * 1024 * 1024
        ),
    )(logit_scale, logit_bias, *pinned)
    return pl.pallas_call(
        write_out,
        out_shape=shapes,
        in_specs=[vmem] * 3,
        out_specs=(hbm,) * 3,
        scratch_shapes=[dma((3,))],
    )(*held)


def solution(mesh):
    in_specs = (
        P(("groups", "row"), "col", None),
        P(("groups", "col"), "row", None),
        P(("groups", "row"), "col", None),
        P(("groups", "row"), "col", None),
        P(),
        P(),
    )
    out_specs = (
        P(("groups", "row"), "col"),
        P(("groups", "row"), "col", None),
        P(("groups", "col"), "row", None),
    )
    body = functools.partial(local, mesh.shape["row"], mesh.shape["col"])
    return jax.shard_map(body, mesh=mesh, in_specs=in_specs, out_specs=out_specs, check_vma=False)
```

```python
import functools

import jax
import jax.numpy as jnp
from jax import lax
from jax.experimental import pallas as pl
from jax.experimental.pallas import tpu as pltpu
from jax.sharding import PartitionSpec as P

NT = (((1,), (1,)), ((), ()))
CHUNKS = 1


def kernel(
    nr, nc, scale_hbm, bias_hbm, pr_hbm, pc_hbm, row_ref, col_ref,
    logit_out, row_out, col_out,
    scale_ref, bias_ref, pr_ref, pc_ref, rows, cols, labels, lt, gt, cp, cp_in, rp, rp_in,
    own_sem, row_send, row_recv, col_send, col_recv, cp_send, cp_recv, rp_send, rp_recv,
):
    g, r, c = lax.axis_index("groups"), lax.axis_index("row"), lax.axis_index("col")
    rs, cs = row_ref.shape[1], col_ref.shape[1]
    depth = row_ref.shape[2]
    rows_tile, cols_tile = rs * nc, cs * nr

    barrier = pltpu.get_barrier_semaphore()
    for k in range(1, nr):
        pl.semaphore_signal(barrier, inc=1, device_id=(g, lax.rem(r + k, nr), c), device_id_type=pl.DeviceIdType.MESH)
    for k in range(1, nc):
        pl.semaphore_signal(barrier, inc=1, device_id=(g, r, lax.rem(c + k, nc)), device_id_type=pl.DeviceIdType.MESH)
    own_row = pltpu.make_async_copy(row_ref.at[0], rows.at[c], own_sem.at[0])
    own_col = pltpu.make_async_copy(col_ref.at[0], cols.at[r], own_sem.at[1])
    small = [
        pltpu.make_async_copy(src, dst, own_sem.at[2 + i])
        for i, (src, dst) in enumerate(
            ((pr_hbm, pr_ref), (pc_hbm, pc_ref), (scale_hbm, scale_ref), (bias_hbm, bias_ref))
        )
    ]
    for copy in [*small, own_row, own_col]:
        copy.start()

    def remote(src, dst, send, recv, where):
        return pltpu.make_async_remote_copy(
            src_ref=src, dst_ref=dst, send_sem=send, recv_sem=recv, device_id=where, device_id_type=pl.DeviceIdType.MESH
        )

    half = nr // 2 if nr % 2 == 0 else nr
    base = r // half * half
    across = lax.rem(r + half, nr)
    near = [base + lax.rem(r - base + k, half) for k in range(1, half)]
    step = cs // CHUNKS

    def other_half(s):
        return lax.rem(s + half, nr)

    def mate(d):
        return d + 1 - 2 * (d % 2)

    def chunk(ref, h):
        return ref.at[pl.ds(h * step, step)]

    def row_copy(to, slot, own):
        src = row_ref.at[0] if own else rows.at[slot]
        return remote(src, rows.at[slot], row_send.at[to if own else mate(slot)], row_recv.at[slot], (g, r, to))

    def col_copy(to, slot, h, own):
        src = col_ref.at[0] if own else cols.at[slot]
        send = col_send.at[to if own else other_half(to), h]
        return remote(chunk(src, h), chunk(cols.at[slot], h), send, col_recv.at[slot, h], (g, to, c))

    def cp_copy(to, slot, h):
        return remote(chunk(cp.at[to], h), chunk(cp_in.at[slot], h), cp_send.at[to, h], cp_recv.at[slot, h], (g, to, c))

    def rp_copy(to, slot):
        return remote(rp.at[to], rp_in.at[slot], rp_send.at[to], rp_recv.at[slot], (g, r, to))

    chips = [lax.rem(c + 2 * k, nc) for k in range(1, nc // 2)]
    pl.semaphore_wait(barrier, nr + nc - 2)
    if half < nr:
        for h in range(CHUNKS):
            col_copy(across, r, h, True).start()
    for to in [*chips, mate(c)]:
        row_copy(to, c, True).start()
    for h in range(CHUNKS):
        for to in near:
            col_copy(to, r, h, True).start()

    for copy in small:
        copy.wait()
    factor, offset = scale_ref[0], bias_ref[0]
    pairs = pr_ref.shape[2]
    hit_rows = (lax.broadcasted_iota(jnp.int32, (rows_tile, pairs), 0) == pr_ref[0]).astype(jnp.bfloat16)
    hit_cols = (lax.broadcasted_iota(jnp.int32, (cols_tile, pairs), 0) == pc_ref[0]).astype(jnp.bfloat16)
    count = lax.dot_general(hit_cols, hit_rows, NT, preferred_element_type=jnp.float32)
    labels[...] = jnp.where(count > 0.5, 1.0, 0.0)

    own_row.wait()
    own_col.wait()
    for s in chips:
        row_copy(c, s, True).wait_recv()
        row_copy(mate(c), s, False).start()

    def block(s, h):
        first = s * cs + h * step
        at = pl.ds(pl.multiple_of(first, step), step)
        row_all = rows[...].reshape(rows_tile, depth)
        part = cols[s, pl.ds(h * step, step)]
        scores = factor * lax.dot_general(part, row_all, NT, preferred_element_type=jnp.float32) + offset
        lt[at, :] = scores
        grad = (jax.nn.sigmoid(scores) - labels[at, :]).astype(jnp.bfloat16)
        gt[at, :] = grad
        return jnp.dot(grad, row_all, preferred_element_type=jnp.float32).astype(jnp.bfloat16)

    def arrived(s, h):
        cp[s, pl.ds(h * step, step)] = block(s, h)
        cp_copy(s, r, h).start()

    def have_rows():
        for s in [c, *chips]:
            row_copy(c, mate(s), True).wait_recv()

    for h in range(CHUNKS):
        if half < nr:
            col_copy(r, across, h, True).wait_recv()
            for to in near:
                col_copy(to, across, h, False).start()
        if h == 0:
            have_rows()
        if half < nr:
            arrived(across, h)

    def from_near(k):
        s = base + lax.rem(r - base + k, half)
        for h in range(CHUNKS):
            col_copy(r, s, h, True).wait_recv()
            arrived(s, h)

    def from_far(k):
        s = other_half(base + lax.rem(r - base + k, half))
        for h in range(CHUNKS):
            col_copy(r, s, h, True).wait_recv()
            arrived(s, h)

    def in_turn(body):
        if half <= 2:
            for k in range(1, half):
                body(k)
        else:
            pl.loop(1, half)(body)

    in_turn(from_near)
    for h in range(CHUNKS):
        cp_in[r, pl.ds(h * step, step)] = block(r, h)
    if half < nr:
        in_turn(from_far)

    cols_all = cols[...].reshape(cols_tile, depth)
    grad = gt[...].T
    out = jnp.dot(grad, cols_all, preferred_element_type=jnp.float32).astype(jnp.bfloat16)
    rp[...] = out.reshape(nc, rs, depth)
    for k in range(1, nc):
        rp_copy(lax.rem(c + k, nc), c).start()
    rp_in[c] = rp[c]
    logit_out[...] = lt[...].T.astype(jnp.bfloat16)

    def total(parts, n):
        add = parts[0].astype(jnp.float32)
        for s in range(1, n):
            add += parts[s].astype(jnp.float32)
        return (factor * add).astype(jnp.bfloat16)

    for k in range(1, nc):
        s = lax.rem(c + k, nc)
        rp_copy(s, s).wait_recv()
    row_out[0] = total(rp_in, nc)
    for k in range(1, nr):
        s = lax.rem(r + k, nr)
        for h in range(CHUNKS):
            cp_copy(s, s, h).wait_recv()
    col_out[0] = total(cp_in, nr)

    for h in range(CHUNKS):
        if half < nr:
            col_copy(across, r, h, True).wait_send()
        for to in near:
            col_copy(to, r, h, True).wait_send()
            if half < nr:
                col_copy(to, across, h, False).wait_send()
        for k in range(1, nr):
            cp_copy(lax.rem(r + k, nr), r, h).wait_send()
    for to in [*chips, mate(c)]:
        row_copy(to, c, True).wait_send()
    for s in chips:
        row_copy(mate(c), s, False).wait_send()
    for k in range(1, nc):
        rp_copy(lax.rem(c + k, nc), c).wait_send()


def local(nr, nc, row_embed, col_embed, pos_rows, pos_cols, logit_scale, logit_bias):
    _, rs, depth = row_embed.shape
    cs = col_embed.shape[1]
    rows_tile, cols_tile = rs * nc, cs * nr
    bf16, f32 = jnp.bfloat16, jnp.float32
    vmem, hbm = (pl.BlockSpec(memory_space=m) for m in (pltpu.VMEM, pltpu.HBM))
    dma = pltpu.SemaphoreType.DMA
    shapes = (
        jax.ShapeDtypeStruct((rows_tile, cols_tile), bf16),
        jax.ShapeDtypeStruct((1, rs, depth), bf16),
        jax.ShapeDtypeStruct((1, cs, depth), bf16),
    )
    operands = (pos_rows, pos_cols, row_embed, col_embed)
    pinned = [pltpu.with_memory_space_constraint(x, pltpu.HBM) for x in operands]
    return pl.pallas_call(
        functools.partial(kernel, nr, nc),
        out_shape=shapes,
        in_specs=[hbm] * 6,
        out_specs=(vmem,) * 3,
        scratch_shapes=[
            pltpu.SMEM((1,), f32),
            pltpu.SMEM((1,), f32),
            pltpu.VMEM(pos_rows.shape, jnp.int32),
            pltpu.VMEM(pos_cols.shape, jnp.int32),
            pltpu.VMEM((nc, rs, depth), bf16),
            pltpu.VMEM((nr, cs, depth), bf16),
            pltpu.VMEM((cols_tile, rows_tile), f32),
            pltpu.VMEM((cols_tile, rows_tile), f32),
            pltpu.VMEM((cols_tile, rows_tile), bf16),
            pltpu.VMEM((nr, cs, depth), bf16),
            pltpu.VMEM((nr, cs, depth), bf16),
            pltpu.VMEM((nc, rs, depth), bf16),
            pltpu.VMEM((nc, rs, depth), bf16),
            dma((6,)),
            dma((nc,)),
            dma((nc,)),
            dma((nr, CHUNKS)),
            dma((nr, CHUNKS)),
            dma((nr, CHUNKS)),
            dma((nr, CHUNKS)),
            dma((nc,)),
            dma((nc,)),
        ],
        compiler_params=pltpu.CompilerParams(
            collective_id=0, has_side_effects=True, vmem_limit_bytes=50 * 1024 * 1024
        ),
    )(logit_scale, logit_bias, *pinned)


def solution(mesh):
    in_specs = (
        P(("groups", "row"), "col", None),
        P(("groups", "col"), "row", None),
        P(("groups", "row"), "col", None),
        P(("groups", "row"), "col", None),
        P(),
        P(),
    )
    out_specs = (
        P(("groups", "row"), "col"),
        P(("groups", "row"), "col", None),
        P(("groups", "col"), "row", None),
    )
    body = functools.partial(local, mesh.shape["row"], mesh.shape["col"])
    return jax.shard_map(body, mesh=mesh, in_specs=in_specs, out_specs=out_specs, check_vma=False)
```

```python
import functools

import jax
import jax.numpy as jnp
from jax import lax
from jax.experimental import pallas as pl
from jax.experimental.pallas import tpu as pltpu
from jax.sharding import PartitionSpec as P

NT = (((1,), (1,)), ((), ()))
CHUNKS = 2


def kernel(
    nr, nc, scale_hbm, bias_hbm, pr_hbm, pc_hbm, row_ref, col_ref,
    logit_out, grads_out,
    scale_ref, bias_ref, pr_ref, pc_ref, rows, cols, labels, lt, gt, cp, cp_in, rp, rp_in,
    own_sem, row_send, row_recv, col_send, col_recv, cp_send, cp_recv, rp_send, rp_recv,
):
    g, r, c = lax.axis_index("groups"), lax.axis_index("row"), lax.axis_index("col")
    rs, cs = row_ref.shape[1], col_ref.shape[1]
    depth = row_ref.shape[2]
    rows_tile, cols_tile = rs * nc, cs * nr

    half = nr // 2 if nr % 2 == 0 else nr
    base = r // half * half
    across = lax.rem(r + half, nr)
    near = [base + lax.rem(r - base + k, half) for k in range(1, half)]
    chips = [lax.rem(c + 2 * k, nc) for k in range(1, nc // 2)]

    def mate(d):
        return d + 1 - 2 * (d % 2)

    first = [(g, lax.rem(r + k, nr), c) for k in range(1, nr)] + [(g, r, lax.rem(c + k, nc)) for k in range(1, nc)]
    barrier = pltpu.get_barrier_semaphore()
    for where in first:
        pl.semaphore_signal(barrier, inc=1, device_id=where, device_id_type=pl.DeviceIdType.MESH)
    own_row = pltpu.make_async_copy(row_ref.at[0], rows.at[c], own_sem.at[0])
    own_col = pltpu.make_async_copy(col_ref.at[0], cols.at[r], own_sem.at[1])
    small = [
        pltpu.make_async_copy(src, dst, own_sem.at[2 + i])
        for i, (src, dst) in enumerate(
            ((pr_hbm, pr_ref), (pc_hbm, pc_ref), (scale_hbm, scale_ref), (bias_hbm, bias_ref))
        )
    ]
    for copy in [*small, own_row, own_col]:
        copy.start()

    def remote(src, dst, send, recv, where):
        return pltpu.make_async_remote_copy(
            src_ref=src, dst_ref=dst, send_sem=send, recv_sem=recv, device_id=where, device_id_type=pl.DeviceIdType.MESH
        )

    step = cs // CHUNKS

    def other_half(s):
        return lax.rem(s + half, nr)

    def chunk(ref, h):
        return ref.at[pl.ds(h * step, step)]

    def row_copy(to, slot, own):
        src = row_ref.at[0] if own else rows.at[slot]
        return remote(src, rows.at[slot], row_send.at[to if own else mate(slot)], row_recv.at[slot], (g, r, to))

    def col_copy(to, slot, h, own):
        src = col_ref.at[0] if own else cols.at[slot]
        send = col_send.at[to if own else other_half(to), h]
        return remote(chunk(src, h), chunk(cols.at[slot], h), send, col_recv.at[slot, h], (g, to, c))

    def cp_copy(to, slot):
        return remote(cp.at[to], cp_in.at[slot], cp_send.at[to, 0], cp_recv.at[slot, 0], (g, to, c))

    def rp_copy(to, slot):
        return remote(rp.at[to], rp_in.at[slot], rp_send.at[to], rp_recv.at[slot], (g, r, to))

    pl.semaphore_wait(barrier, len(first))
    if half < nr:
        for h in range(CHUNKS):
            col_copy(across, r, h, True).start()
    for to in [*chips, mate(c)]:
        row_copy(to, c, True).start()
    for h in range(CHUNKS):
        for to in near:
            col_copy(to, r, h, True).start()

    for copy in small:
        copy.wait()
    factor, offset = scale_ref[0], bias_ref[0]
    pairs = pr_ref.shape[2]
    hit_rows = (lax.broadcasted_iota(jnp.int32, (rows_tile, pairs), 0) == pr_ref[0]).astype(jnp.bfloat16)
    hit_cols = (lax.broadcasted_iota(jnp.int32, (cols_tile, pairs), 0) == pc_ref[0]).astype(jnp.bfloat16)
    count = lax.dot_general(hit_cols, hit_rows, NT, preferred_element_type=jnp.float32)
    labels[...] = jnp.where(count > 0.5, 1.0, 0.0)

    own_row.wait()
    own_col.wait()
    for s in chips:
        row_copy(c, s, True).wait_recv()
        row_copy(mate(c), s, False).start()

    def block(s):
        at = pl.ds(pl.multiple_of(s * cs, cs), cs)
        row_all = rows[...].reshape(rows_tile, depth)
        scores = factor * lax.dot_general(cols[s], row_all, NT, preferred_element_type=jnp.float32) + offset
        lt[at, :] = scores
        grad = (jax.nn.sigmoid(scores) - labels[at, :]).astype(jnp.bfloat16)
        gt[at, :] = grad
        return jnp.dot(grad, row_all, preferred_element_type=jnp.float32).astype(jnp.bfloat16)

    if half < nr:
        for h in range(CHUNKS):
            col_copy(r, across, h, True).wait_recv()
            for to in near:
                col_copy(to, across, h, False).start()
    for s in [c, *chips]:
        row_copy(c, mate(s), True).wait_recv()
    if half < nr:
        cp[across] = block(across)
        cp_copy(across, r).start()

    def from_near(k):
        s = base + lax.rem(r - base + k, half)
        for h in range(CHUNKS):
            col_copy(r, s, h, True).wait_recv()
        cp[s] = block(s)

    def from_far(k):
        s = other_half(base + lax.rem(r - base + k, half))
        for h in range(CHUNKS):
            col_copy(r, s, h, True).wait_recv()
        cp[s] = block(s)
        cp_copy(s, r).start()

    def in_turn(body):
        if half <= 2:
            for k in range(1, half):
                body(k)
        else:
            pl.loop(1, half)(body)

    in_turn(from_near)
    cp_in[r] = block(r)
    if half < nr:
        in_turn(from_far)
    for to in near:
        cp_copy(to, r).start()

    cols_all = cols[...].reshape(cols_tile, depth)
    grad = gt[...].T
    out = jnp.dot(grad, cols_all, preferred_element_type=jnp.float32).astype(jnp.bfloat16)
    rp[...] = out.reshape(nc, rs, depth)
    for k in range(1, nc):
        rp_copy(lax.rem(c + k, nc), c).start()
    rp_in[c] = rp[c]
    logit_out[...] = lt[...].T.astype(jnp.bfloat16)

    def total(parts, n):
        add = parts[0].astype(jnp.float32)
        for s in range(1, n):
            add += parts[s].astype(jnp.float32)
        return (factor * add).astype(jnp.bfloat16)

    for k in range(1, nc):
        s = lax.rem(c + k, nc)
        rp_copy(s, s).wait_recv()
    grads_out[pl.ds(0, rs)] = total(rp_in, nc)
    for k in range(1, nr):
        s = lax.rem(r + k, nr)
        cp_copy(s, s).wait_recv()
    grads_out[pl.ds(rs, cs)] = total(cp_in, nr)

    for h in range(CHUNKS):
        if half < nr:
            col_copy(across, r, h, True).wait_send()
        for to in near:
            col_copy(to, r, h, True).wait_send()
            if half < nr:
                col_copy(to, across, h, False).wait_send()
    for k in range(1, nr):
        cp_copy(lax.rem(r + k, nr), r).wait_send()
    for to in [*chips, mate(c)]:
        row_copy(to, c, True).wait_send()
    for s in chips:
        row_copy(mate(c), s, False).wait_send()
    for k in range(1, nc):
        rp_copy(lax.rem(c + k, nc), c).wait_send()


def local(nr, nc, row_embed, col_embed, pos_rows, pos_cols, logit_scale, logit_bias):
    _, rs, depth = row_embed.shape
    cs = col_embed.shape[1]
    rows_tile, cols_tile = rs * nc, cs * nr
    bf16, f32 = jnp.bfloat16, jnp.float32
    vmem, hbm = (pl.BlockSpec(memory_space=m) for m in (pltpu.VMEM, pltpu.HBM))
    dma = pltpu.SemaphoreType.DMA
    shapes = (
        jax.ShapeDtypeStruct((rows_tile, cols_tile), bf16),
        jax.ShapeDtypeStruct((rs + cs, depth), bf16),
    )
    operands = (pos_rows, pos_cols, row_embed, col_embed)
    pinned = [pltpu.with_memory_space_constraint(x, pltpu.HBM) for x in operands]
    logits, grads = pl.pallas_call(
        functools.partial(kernel, nr, nc),
        out_shape=shapes,
        in_specs=[hbm] * 6,
        out_specs=(vmem,) * 2,
        scratch_shapes=[
            pltpu.SMEM((1,), f32),
            pltpu.SMEM((1,), f32),
            pltpu.VMEM(pos_rows.shape, jnp.int32),
            pltpu.VMEM(pos_cols.shape, jnp.int32),
            pltpu.VMEM((nc, rs, depth), bf16),
            pltpu.VMEM((nr, cs, depth), bf16),
            pltpu.VMEM((cols_tile, rows_tile), f32),
            pltpu.VMEM((cols_tile, rows_tile), f32),
            pltpu.VMEM((cols_tile, rows_tile), bf16),
            pltpu.VMEM((nr, cs, depth), bf16),
            pltpu.VMEM((nr, cs, depth), bf16),
            pltpu.VMEM((nc, rs, depth), bf16),
            pltpu.VMEM((nc, rs, depth), bf16),
            dma((6,)),
            dma((nc,)),
            dma((nc,)),
            dma((nr, CHUNKS)),
            dma((nr, CHUNKS)),
            dma((nr, CHUNKS)),
            dma((nr, CHUNKS)),
            dma((nc,)),
            dma((nc,)),
        ],
        compiler_params=pltpu.CompilerParams(
            collective_id=0, has_side_effects=True, vmem_limit_bytes=50 * 1024 * 1024
        ),
    )(logit_scale, logit_bias, *pinned)
    return logits, grads[None, :rs], grads[None, rs:]


def solution(mesh):
    in_specs = (
        P(("groups", "row"), "col", None),
        P(("groups", "col"), "row", None),
        P(("groups", "row"), "col", None),
        P(("groups", "row"), "col", None),
        P(),
        P(),
    )
    out_specs = (
        P(("groups", "row"), "col"),
        P(("groups", "row"), "col", None),
        P(("groups", "col"), "row", None),
    )
    body = functools.partial(local, mesh.shape["row"], mesh.shape["col"])
    return jax.shard_map(body, mesh=mesh, in_specs=in_specs, out_specs=out_specs, check_vma=False)
```

```python
import functools

import jax
import jax.numpy as jnp
from jax import lax
from jax.experimental import pallas as pl
from jax.experimental.pallas import tpu as pltpu
from jax.sharding import PartitionSpec as P

NT = (((1,), (1,)), ((), ()))
CHUNKS = 1


def kernel(
    nr, nc, scale_hbm, bias_hbm, pr_hbm, pc_hbm, row_ref, col_ref,
    logit_out, grads_out,
    scale_ref, bias_ref, pr_ref, pc_ref, rows, cols, labels, lt, gt, cp, cp_in, rp, rp_in,
    own_sem, row_send, row_recv, col_send, col_recv, cp_send, cp_recv, rp_send, rp_recv,
):
    g, r, c = lax.axis_index("groups"), lax.axis_index("row"), lax.axis_index("col")
    rs, cs = row_ref.shape[1], col_ref.shape[1]
    depth = row_ref.shape[2]
    rows_tile, cols_tile = rs * nc, cs * nr

    half = nr // 2 if nr % 2 == 0 else nr
    base = r // half * half
    across = nr - 1 - r
    near = [base + lax.rem(r - base + k, half) for k in range(1, half)]
    chips = [lax.rem(c + 2 * k, nc) for k in range(1, nc // 2)]

    def mate(d):
        return d + 1 - 2 * (d % 2)

    first = [(g, lax.rem(r + k, nr), c) for k in range(1, nr)] + [(g, r, lax.rem(c + k, nc)) for k in range(1, nc)]
    barrier = pltpu.get_barrier_semaphore()
    for where in first:
        pl.semaphore_signal(barrier, inc=1, device_id=where, device_id_type=pl.DeviceIdType.MESH)
    own_row = pltpu.make_async_copy(row_ref.at[0], rows.at[c], own_sem.at[0])
    own_col = pltpu.make_async_copy(col_ref.at[0], cols.at[r], own_sem.at[1])
    small = [
        pltpu.make_async_copy(src, dst, own_sem.at[2 + i])
        for i, (src, dst) in enumerate(
            ((pr_hbm, pr_ref), (pc_hbm, pc_ref), (scale_hbm, scale_ref), (bias_hbm, bias_ref))
        )
    ]
    for copy in [*small, own_row, own_col]:
        copy.start()

    def remote(src, dst, send, recv, where):
        return pltpu.make_async_remote_copy(
            src_ref=src, dst_ref=dst, send_sem=send, recv_sem=recv, device_id=where, device_id_type=pl.DeviceIdType.MESH
        )

    step = cs // CHUNKS

    def other_half(s):
        return nr - 1 - s

    def chunk(ref, h):
        return ref.at[pl.ds(h * step, step)]

    def row_copy(to, slot, own):
        src = row_ref.at[0] if own else rows.at[slot]
        return remote(src, rows.at[slot], row_send.at[to if own else mate(slot)], row_recv.at[slot], (g, r, to))

    def col_copy(to, slot, h, own):
        src = col_ref.at[0] if own else cols.at[slot]
        send = col_send.at[to if own else other_half(to), h]
        return remote(chunk(src, h), chunk(cols.at[slot], h), send, col_recv.at[slot, h], (g, to, c))

    def cp_copy(to, slot):
        return remote(cp.at[to], cp_in.at[slot], cp_send.at[to, 0], cp_recv.at[slot, 0], (g, to, c))

    def rp_copy(to, slot):
        return remote(rp.at[to], rp_in.at[slot], rp_send.at[to], rp_recv.at[slot], (g, r, to))

    pl.semaphore_wait(barrier, len(first))
    if half < nr:
        for h in range(CHUNKS):
            col_copy(across, r, h, True).start()
    for to in [*chips, mate(c)]:
        row_copy(to, c, True).start()
    for h in range(CHUNKS):
        for to in near:
            col_copy(to, r, h, True).start()

    for copy in small:
        copy.wait()
    factor, offset = scale_ref[0], bias_ref[0]
    pairs = pr_ref.shape[2]
    hit_rows = (lax.broadcasted_iota(jnp.int32, (rows_tile, pairs), 0) == pr_ref[0]).astype(jnp.bfloat16)
    hit_cols = (lax.broadcasted_iota(jnp.int32, (cols_tile, pairs), 0) == pc_ref[0]).astype(jnp.bfloat16)
    count = lax.dot_general(hit_cols, hit_rows, NT, preferred_element_type=jnp.float32)
    labels[...] = jnp.where(count > 0.5, 1.0, 0.0)

    own_row.wait()
    own_col.wait()
    for s in chips:
        row_copy(c, s, True).wait_recv()
        row_copy(mate(c), s, False).start()

    def block(s):
        at = pl.ds(pl.multiple_of(s * cs, cs), cs)
        row_all = rows[...].reshape(rows_tile, depth)
        scores = factor * lax.dot_general(cols[s], row_all, NT, preferred_element_type=jnp.float32) + offset
        lt[at, :] = scores
        grad = (jax.nn.sigmoid(scores) - labels[at, :]).astype(jnp.bfloat16)
        gt[at, :] = grad
        return jnp.dot(grad, row_all, preferred_element_type=jnp.float32).astype(jnp.bfloat16)

    if half < nr:
        for h in range(CHUNKS):
            col_copy(r, across, h, True).wait_recv()
            for to in near:
                col_copy(to, across, h, False).start()
    for s in [c, *chips]:
        row_copy(c, mate(s), True).wait_recv()
    if half < nr:
        cp[across] = block(across)
        cp_copy(across, r).start()

    def from_near(k):
        s = base + lax.rem(r - base + k, half)
        for h in range(CHUNKS):
            col_copy(r, s, h, True).wait_recv()
        cp[s] = block(s)

    def from_far(k):
        s = other_half(base + lax.rem(r - base + k, half))
        for h in range(CHUNKS):
            col_copy(r, s, h, True).wait_recv()
        cp[s] = block(s)
        cp_copy(s, r).start()

    def in_turn(body):
        if half <= 2:
            for k in range(1, half):
                body(k)
        else:
            pl.loop(1, half)(body)

    in_turn(from_near)
    cp_in[r] = block(r)
    if half < nr:
        in_turn(from_far)
    for to in near:
        cp_copy(to, r).start()

    cols_all = cols[...].reshape(cols_tile, depth)
    grad = gt[...].T
    out = jnp.dot(grad, cols_all, preferred_element_type=jnp.float32).astype(jnp.bfloat16)
    rp[...] = out.reshape(nc, rs, depth)
    for k in range(1, nc):
        rp_copy(lax.rem(c + k, nc), c).start()
    rp_in[c] = rp[c]
    logit_out[...] = lt[...].T.astype(jnp.bfloat16)

    def total(parts, n):
        add = parts[0].astype(jnp.float32)
        for s in range(1, n):
            add += parts[s].astype(jnp.float32)
        return (factor * add).astype(jnp.bfloat16)

    for k in range(1, nc):
        s = lax.rem(c + k, nc)
        rp_copy(s, s).wait_recv()
    grads_out[pl.ds(0, rs)] = total(rp_in, nc)
    for k in range(1, nr):
        s = lax.rem(r + k, nr)
        cp_copy(s, s).wait_recv()
    grads_out[pl.ds(rs, cs)] = total(cp_in, nr)

    for h in range(CHUNKS):
        if half < nr:
            col_copy(across, r, h, True).wait_send()
        for to in near:
            col_copy(to, r, h, True).wait_send()
            if half < nr:
                col_copy(to, across, h, False).wait_send()
    for k in range(1, nr):
        cp_copy(lax.rem(r + k, nr), r).wait_send()
    for to in [*chips, mate(c)]:
        row_copy(to, c, True).wait_send()
    for s in chips:
        row_copy(mate(c), s, False).wait_send()
    for k in range(1, nc):
        rp_copy(lax.rem(c + k, nc), c).wait_send()


def local(nr, nc, row_embed, col_embed, pos_rows, pos_cols, logit_scale, logit_bias):
    _, rs, depth = row_embed.shape
    cs = col_embed.shape[1]
    rows_tile, cols_tile = rs * nc, cs * nr
    bf16, f32 = jnp.bfloat16, jnp.float32
    vmem, hbm = (pl.BlockSpec(memory_space=m) for m in (pltpu.VMEM, pltpu.HBM))
    dma = pltpu.SemaphoreType.DMA
    shapes = (
        jax.ShapeDtypeStruct((rows_tile, cols_tile), bf16),
        jax.ShapeDtypeStruct((rs + cs, depth), bf16),
    )
    operands = (pos_rows, pos_cols, row_embed, col_embed)
    pinned = [pltpu.with_memory_space_constraint(x, pltpu.HBM) for x in operands]
    logits, grads = pl.pallas_call(
        functools.partial(kernel, nr, nc),
        out_shape=shapes,
        in_specs=[hbm] * 6,
        out_specs=(vmem,) * 2,
        scratch_shapes=[
            pltpu.SMEM((1,), f32),
            pltpu.SMEM((1,), f32),
            pltpu.VMEM(pos_rows.shape, jnp.int32),
            pltpu.VMEM(pos_cols.shape, jnp.int32),
            pltpu.VMEM((nc, rs, depth), bf16),
            pltpu.VMEM((nr, cs, depth), bf16),
            pltpu.VMEM((cols_tile, rows_tile), f32),
            pltpu.VMEM((cols_tile, rows_tile), f32),
            pltpu.VMEM((cols_tile, rows_tile), bf16),
            pltpu.VMEM((nr, cs, depth), bf16),
            pltpu.VMEM((nr, cs, depth), bf16),
            pltpu.VMEM((nc, rs, depth), bf16),
            pltpu.VMEM((nc, rs, depth), bf16),
            dma((6,)),
            dma((nc,)),
            dma((nc,)),
            dma((nr, CHUNKS)),
            dma((nr, CHUNKS)),
            dma((nr, CHUNKS)),
            dma((nr, CHUNKS)),
            dma((nc,)),
            dma((nc,)),
        ],
        compiler_params=pltpu.CompilerParams(
            collective_id=0, has_side_effects=True, vmem_limit_bytes=50 * 1024 * 1024
        ),
    )(logit_scale, logit_bias, *pinned)
    return logits, grads[None, :rs], grads[None, rs:]


def solution(mesh):
    in_specs = (
        P(("groups", "row"), "col", None),
        P(("groups", "col"), "row", None),
        P(("groups", "row"), "col", None),
        P(("groups", "row"), "col", None),
        P(),
        P(),
    )
    out_specs = (
        P(("groups", "row"), "col"),
        P(("groups", "row"), "col", None),
        P(("groups", "col"), "row", None),
    )
    body = functools.partial(local, mesh.shape["row"], mesh.shape["col"])
    return jax.shard_map(body, mesh=mesh, in_specs=in_specs, out_specs=out_specs, check_vma=False)
```
